512 devices in a mesh: leaf: 32 (over x, y), tile: 16 (over z, core).
Axes of the slice: x: 4, y: 8, z: 8, core: 2. Of those that a mesh axis runs over, the one named last changes fastest.
Arguments:
- parent_cov: float32 [4, 2048, 2048], P(None, 'tile', 'leaf'), as said below
- parent_map: int32 [32], P('leaf'), may hold values from 0 to 3
- front_rows: int32 [32, 2], P('leaf'), may hold values from 1024 to 1536, as said below
- rows_mid: int32 [32, 1536], P('leaf'), may hold values from 0 to 2047, as said below
- rows_low: int32 [32, 1536], P('leaf'), may hold values from 0 to 2047, as said below
- factor_mid: float32 [32, 1536, 512], P('leaf', 'tile'), may hold values from -0.15625 to 0.15625
- dinv_mid: float32 [32, 512, 512], P('leaf', 'tile'), as said below
- factor_low: float32 [32, 1536, 512], P('leaf', 'tile'), may hold values from -0.15625 to 0.15625
- diag_low: float32 [32, 512], P('leaf', 'tile'), may hold values from 0.5 to 2
Outputs:
- variance_mid: float32 [32, 512], P('leaf', 'tile')
- variance_low: float32 [32, 512], P('leaf', 'tile')
The draws below stay inside these ranges and needn't reach their ends.
Inputs may be any that keep to these rules, and one draw needn't show every extreme that they name: Each parent_cov[p] is exactly symmetric. Each dinv_mid[g] is exactly symmetric. `front_rows`: some group has 1536 live rows in both columns. `rows_mid`: each row holds 1536 distinct positions in increasing order. `rows_low`: row g holds 1536 distinct positions in increasing order, all below 512 + front_rows[g, 0].
All inputs are finite; a program needn't handle non-finite values.
Results may differ from the reference program's by a relative error of at most 0.0003.
Values sent between devices are 32-bit elements; how exact they have to be, the bound alone decides.
A program may use at most 64 MiB of HBM per device.

```python
import math
import jax
import jax.numpy as jnp
from jax import lax

S = 512
M = 1536
NPAR = 4
F = 2048
GROUPS = 32
N_LEAF = 32


def symmetric_blocks(key, number, order):
    first_key, second_key = jax.random.split(key, 2)
    base = jax.random.normal(first_key, (number, order, order), jnp.float32)
    offdiag = (base + jnp.swapaxes(base, 1, 2)) * (0.3 / math.sqrt(order))
    diagonal = jax.random.uniform(second_key, (number, order), jnp.float32, 1.0, 2.0)
    identity = jnp.eye(order, dtype=jnp.float32)
    whole = offdiag + identity[None, :, :] * diagonal[:, None, :]
    return whole


def live_counts(key):
    count_key, group_key = jax.random.split(jax.random.fold_in(key, 17))
    counts = jax.random.randint(count_key, (N_LEAF, 2), M * 2 // 3, M + 1)
    full_group = jax.random.randint(group_key, (), 0, N_LEAF)
    counts = counts.at[full_group].set(M)
    return counts.astype(jnp.int32)


def pick_positions(key, bound):
    shuffled = jax.random.permutation(key, F).astype(jnp.int32)
    special = jnp.logical_or(shuffled == 0, shuffled == bound - 1)
    rank_key = jnp.where(special, 0, jnp.where(shuffled < bound, 1, 2)).astype(jnp.int32)
    ranking = jnp.argsort(rank_key, stable=True)
    return jnp.sort(shuffled[ranking][:M]).astype(jnp.int32)


def draw_parent_cov(key, part):
    return symmetric_blocks(jax.random.fold_in(key, 3), NPAR, F)


def draw_dinv_mid(key, part):
    return symmetric_blocks(jax.random.fold_in(key, 5), N_LEAF, S)


def draw_front_rows(key, part):
    return live_counts(key)


def draw_rows_mid(key, part):
    group_keys = jax.random.split(jax.random.fold_in(key, 23), N_LEAF)
    bounds = jnp.full((N_LEAF,), F, jnp.int32)
    return jax.vmap(pick_positions)(group_keys, bounds)


def draw_rows_low(key, part):
    counts = live_counts(key)
    group_keys = jax.random.split(jax.random.fold_in(key, 29), N_LEAF)
    bounds = (S + counts[:, 0]).astype(jnp.int32)
    return jax.vmap(pick_positions)(group_keys, bounds)


def with_ends(entries, key, least, top_value):
    shape = entries.shape
    place = [jax.random.randint(jax.random.fold_in(key, axis), (), 0, shape[axis]) for axis in range(len(shape))]
    entries = entries.at[tuple(place)].set(least)
    longest = shape.index(max(shape))
    place[longest] = (place[longest] + 1) % shape[longest]
    return entries.at[tuple(place)].set(top_value)


def level_of(key, extent, cuts, least, largest):
    def one(position, blocks):
        draws = jax.random.uniform(jax.random.fold_in(jax.random.fold_in(key, 6), position), (blocks,), jnp.float32, least / len(cuts), largest / len(cuts))
        return jnp.repeat(jnp.exp(draws), extent[position] // blocks).reshape((-1,) + (1,) * (len(extent) - position - 1))

    factor_of = one(*cuts[0])
    for cut in cuts[1:]:
        factor_of = factor_of * one(*cut)
    return factor_of


def bell_draw(stream_key, extent, spread, limit, pieces=(), kind=jnp.bfloat16):
    result = jax.random.normal(stream_key, extent, jnp.float32) * spread
    if len(pieces) > 0:
        result = level_of(stream_key, extent, pieces, -0.22, 0.18) * result
    return jnp.clip(result, min=-limit, max=limit).astype(kind)


def setup_inputs(seed: int = 0) -> dict:
    key_of = jax.random.split(jax.random.key(seed), 10)
    return {
        "parent_cov": draw_parent_cov(jax.random.fold_in(key_of[9], 71), 0),
        "parent_map": with_ends(jax.random.randint(key_of[1], (GROUPS,), 0, NPAR), jax.random.fold_in(key_of[1], 1), 0, NPAR - 1).astype(jnp.int32),
        "front_rows": draw_front_rows(jax.random.fold_in(key_of[9], 71), 0),
        "rows_mid": draw_rows_mid(jax.random.fold_in(key_of[9], 71), 0),
        "rows_low": draw_rows_low(jax.random.fold_in(key_of[9], 71), 0),
        "factor_mid": bell_draw(key_of[5], (GROUPS, M, S), M ** -0.5, 0.15625, ((0, 32), (1, 16)), jnp.float32),
        "dinv_mid": draw_dinv_mid(jax.random.fold_in(key_of[9], 71), 0),
        "factor_low": bell_draw(key_of[7], (GROUPS, M, S), M ** -0.5, 0.15625, ((0, 32), (1, 16)), jnp.float32),
        "diag_low": jnp.clip(jnp.exp(math.log(2.0) - 1.3862944 * jax.random.uniform(key_of[8], (GROUPS, S), jnp.float32) ** level_of(key_of[8], (GROUPS, S), ((0, 32), (1, 16)), -0.2, 0.2)), 0.5, 2.0),
    }


EXACT_PRECISION = lax.Precision.HIGHEST


def restrict(matrix, positions, live_count):
    live_mask = (jnp.arange(positions.shape[0]) < live_count).astype(matrix.dtype)
    picked = jnp.take(jnp.take(matrix, positions, axis=0), positions, axis=1)
    return picked * live_mask[:, None] * live_mask[None, :]


def reference(parent_cov, parent_map, front_rows, rows_mid, rows_low, factor_mid, dinv_mid, factor_low, diag_low):
    def one_group(inputs):
        parent_index, counts, mid_list, low_list, factor_m, dinv_m, factor_l, diag_l = inputs
        parent = lax.dynamic_index_in_dim(parent_cov, parent_index, 0, keepdims=False)
        mid_block = restrict(parent, mid_list, counts[0])
        mid_cross = -jnp.dot(mid_block, factor_m, precision=EXACT_PRECISION, preferred_element_type=jnp.float32)
        mid_diag = dinv_m - jnp.dot(factor_m.T, mid_cross, precision=EXACT_PRECISION, preferred_element_type=jnp.float32)
        upper_rows = jnp.concatenate([mid_diag, mid_cross.T], axis=1)
        lower_rows = jnp.concatenate([mid_cross, mid_block], axis=1)
        front = jnp.concatenate([upper_rows, lower_rows], axis=0)
        low_block = restrict(front, low_list, counts[1])
        low_cross = -jnp.dot(low_block, factor_l, precision=EXACT_PRECISION, preferred_element_type=jnp.float32)
        return jnp.diagonal(mid_diag), diag_l - jnp.sum(factor_l * low_cross, axis=0)

    variance_mid, variance_low = lax.map(one_group, (parent_map, front_rows, rows_mid, rows_low, factor_mid, dinv_mid, factor_low, diag_low))
    return (variance_mid, variance_low)
```

```python
import jax
import jax.numpy as jnp
from jax import lax
from jax.experimental import pallas as pl
from jax.experimental.pallas import tpu as pltpu
from jax.sharding import PartitionSpec as P

NX, NY, NZ, NC = 4, 8, 8, 2
NT = NZ * NC
S, M, F = 512, 1536, 2048
RB = F // NT
RF = M // NT
RK = S // NT
HB = RB // 2
CB = F // (NX * NY)
WIN, BLK = 768, 256
NB = M // BLK
BF, F32 = jnp.bfloat16, jnp.float32
MESH = pl.DeviceIdType.MESH

TOP, BOT, DI, ID, TOPL, BOTL, DIL, ROWS = 0, RB, 2 * RB, 2 * RB + RK, 2 * RB + 2 * RK, 3 * RB + 2 * RK, 4 * RB + 2 * RK, 4 * RB + 3 * RK


def split(v):
    hi = v.astype(BF)
    return hi, (v - hi.astype(F32)).astype(BF)


def dot(a, b):
    return jnp.dot(a, b, preferred_element_type=F32)


def kernel(
    cov, pmap, counts, rows_mid, rows_low, fm, dinv, fl, dlow,
    out_mid, out_low,
    ygath, stage, covsel, pmbuf, xm, xl, qoh, roh, csrc, u, v, fhi, flo, fin,
    y_send, y_recv, x_send, x_recv, p_send, p_recv, z_send, z_recv, c_send, c_recv, f_send, f_recv, l_sem,
):
    leaf, tile = lax.axis_index("leaf"), lax.axis_index("tile")
    x, y = leaf // NY, leaf % NY
    z, c = tile // NC, tile % NC

    def leaf_at(dx, dy):
        return lax.rem(x + dx + NX, NX) * NY + lax.rem(y + dy + NY, NY)

    def zt(dz, core=None):
        return lax.rem(z + dz + NZ, NZ) * NC + (c if core is None else core)

    sibling = z * NC + (1 - c)
    up, down = zt(1), zt(-1)
    ynext, yprev = leaf_at(0, 1), leaf_at(0, -1)

    barrier = pltpu.get_barrier_semaphore()
    for d in range(1, NT):
        pl.semaphore_signal(barrier, inc=1, device_id=(leaf, lax.rem(tile + d, NT)), device_id_type=MESH)
    for other in (ynext, yprev, leaf_at(1, 0), leaf_at(2, 0), leaf_at(3, 0)):
        pl.semaphore_signal(barrier, inc=1, device_id=(other, tile), device_id_type=MESH)

    for p in range(4):
        ygath[y, p] = jnp.concatenate([cov[p, :HB, :], cov[p, HB:, :]], axis=1)
    pmbuf[x] = jnp.full((8, 128), pmap[0], jnp.int32)
    pl.semaphore_wait(barrier, NT - 1 + 5)

    def send(src, dst, ssem, rsem, where):
        pltpu.make_async_remote_copy(
            src_ref=src, dst_ref=dst, send_sem=ssem, recv_sem=rsem, device_id=where, device_id_type=MESH
        ).start()

    def wait(ref, sem):
        pltpu.make_async_copy(ref, ref, sem).wait()

    for dx in (1, 2, 3):
        send(pmbuf.at[x], pmbuf.at[x], p_send, p_recv, (leaf_at(dx, 0), tile))
    send(ygath.at[y], ygath.at[y], y_send, y_recv.at[0, 0], (ynext, tile))
    send(ygath.at[y], ygath.at[y], y_send, y_recv.at[1, 0], (yprev, tile))
    facs = ((fm, xm), (fl, xl))
    for a, (own, whole) in enumerate(facs):
        send(own, whole.at[tile], z_send.at[a], z_recv.at[a, 0, 0], (leaf, up))
        send(own, whole.at[tile], z_send.at[a], z_recv.at[a, 1, 0], (leaf, down))
        send(own, whole.at[tile], c_send.at[a], c_recv.at[a], (leaf, sibling))
        pltpu.make_async_copy(own, whole.at[tile], l_sem.at[a]).start()

    live_mid, live_low = counts[0, 0], counts[0, 1]
    lane = lax.broadcasted_iota(jnp.int32, (1, M), 1)
    midv = jnp.where(lane < live_mid, rows_mid[...], -1)
    lowv = jnp.where(lane < live_low, rows_low[...], -1)
    for b in range(NB):
        cols = slice(b * BLK, (b + 1) * BLK)
        pos = lax.broadcasted_iota(jnp.int32, (WIN, BLK), 0) + b * BLK
        qoh[b] = (pos == midv[:, cols]).astype(F32).astype(BF)
        roh[b] = (pos == lowv[:, cols]).astype(F32).astype(BF)
    u[BOT : BOT + RB, S:] = (lax.broadcasted_iota(jnp.int32, (RB, M), 0) + tile * RB == midv).astype(F32).astype(BF)
    dhi, dlo = split(dinv[...])
    eye = lax.broadcasted_iota(jnp.int32, (RK, S), 0) + tile * RK == lax.broadcasted_iota(jnp.int32, (RK, S), 1)
    u[DI : DI + RK, :S] = dhi
    u[ID : ID + RK, :S] = eye.astype(F32).astype(BF)
    u[DIL : DIL + RK, :S] = dlo
    for r0, n in ((DI, 2 * RK), (BOTL, RB + RK)):
        u[r0 : r0 + n, S : 2 * S] = jnp.zeros((n, S), BF)

    wait(pmbuf.at[pl.ds(0, 3)], p_recv)

    def choose(ys):
        for dx in range(NX):
            pm = jnp.broadcast_to(pmbuf[lax.rem(x + dx, NX)][0:1], (HB, 128))
            got = jnp.where(
                pm < 2,
                jnp.where(pm == 0, ygath[ys, 0], ygath[ys, 1]),
                jnp.where(pm == 2, ygath[ys, 2], ygath[ys, 3]),
            )
            if dx == 0:
                covsel[x * NY + ys] = got
            else:
                stage[dx - 1, ys] = got
                send(stage.at[dx - 1, ys], covsel.at[x * NY + ys], x_send, x_recv, (leaf_at(dx, 0), tile))

    choose(y)
    HR = RF // 2
    for s in range(1, 5):
        yb, ya = lax.rem(y + NY - s, NY), lax.rem(y + s, NY)
        if s < 4:
            wait(ygath.at[yb], y_recv.at[0, s - 1])
            wait(ygath.at[ya], y_recv.at[1, s - 1])
            if s < 3:
                send(ygath.at[yb], ygath.at[yb], y_send, y_recv.at[0, s], (ynext, tile))
                send(ygath.at[ya], ygath.at[ya], y_send, y_recv.at[1, s], (yprev, tile))
            else:
                lo, hi = pl.ds(0, 2), pl.ds(2, 2)
                send(ygath.at[yb, lo], ygath.at[yb, lo], y_send, y_recv.at[0, s], (ynext, tile))
                send(ygath.at[ya, hi], ygath.at[ya, hi], y_send, y_recv.at[1, s], (yprev, tile))
            choose(yb)
            choose(ya)
        else:
            wait(ygath.at[yb, pl.ds(0, 2)], y_recv.at[0, s - 1])
            wait(ygath.at[yb, pl.ds(2, 2)], y_recv.at[1, s - 1])
            choose(yb)
        for a, (_, whole) in enumerate(facs):
            tb, ta = zt(-s), zt(s)
            if s < 4:
                wait(whole.at[tb], z_recv.at[a, 0, s - 1])
                wait(whole.at[ta], z_recv.at[a, 1, s - 1])
                if s < 3:
                    send(whole.at[tb], whole.at[tb], z_send.at[a], z_recv.at[a, 0, s], (leaf, up))
                    send(whole.at[ta], whole.at[ta], z_send.at[a], z_recv.at[a, 1, s], (leaf, down))
                else:
                    lo, hi = pl.ds(0, HR), pl.ds(HR, HR)
                    send(whole.at[tb, lo], whole.at[tb, lo], z_send.at[a], z_recv.at[a, 0, s], (leaf, up))
                    send(whole.at[ta, hi], whole.at[ta, hi], z_send.at[a], z_recv.at[a, 1, s], (leaf, down))
                send(whole.at[tb], whole.at[tb], c_send.at[a], c_recv.at[a], (leaf, sibling))
                send(whole.at[ta], whole.at[ta], c_send.at[a], c_recv.at[a], (leaf, sibling))
            else:
                wait(whole.at[tb, pl.ds(0, HR)], z_recv.at[a, 0, s - 1])
                wait(whole.at[tb, pl.ds(HR, HR)], z_recv.at[a, 1, s - 1])
                send(whole.at[tb], whole.at[tb], c_send.at[a], c_recv.at[a], (leaf, sibling))

    wait(covsel.at[pl.ds(0, (NX - 1) * NY)], x_recv)
    low_half = lax.broadcasted_iota(jnp.int32, (HB, 128), 1) < CB
    for m in range(F // 128):
        a, b = covsel[2 * m], covsel[2 * m + 1]
        ra, rb = pltpu.roll(a, CB, 1), pltpu.roll(b, CB, 1)
        for r0, val in ((0, jnp.where(low_half, a, rb)), (HB, jnp.where(low_half, ra, b))):
            hi, lo = split(val)
            csrc[r0 : r0 + HB, m * 128 : (m + 1) * 128] = hi
            csrc[RB + r0 : RB + r0 + HB, m * 128 : (m + 1) * 128] = lo
    for b in range(NB):
        got = dot(csrc[:, b * BLK : b * BLK + WIN], qoh[b]).astype(BF)
        u[TOP : TOP + RB, S + b * BLK : S + (b + 1) * BLK] = got[:RB]
        u[TOPL : TOPL + RB, S + b * BLK : S + (b + 1) * BLK] = got[RB:]

    def pick(r0, n, b):
        cols = slice(b * BLK, (b + 1) * BLK)
        v[r0 : r0 + n, cols] = dot(u[r0 : r0 + n, b * BLK : b * BLK + WIN], roh[b]).astype(BF)

    for b in range(2, NB):
        pick(TOP, 2 * RB, b)
        pick(TOPL, RB, b)

    def halves(a, whole):
        wait(whole.at[tile], l_sem.at[a])
        wait(whole.at[pl.ds(0, NZ)], c_recv.at[a])
        for t in range(NT):
            hi, lo = split(whole[t])
            fhi[t * RF : (t + 1) * RF] = hi
            flo[t * RF : (t + 1) * RF] = lo

    halves(0, xm)
    both = dot(u[TOP : TOP + 2 * RB, S:], fhi[...]) + dot(u[TOP : TOP + 2 * RB, S:], flo[...])
    cross = both[:RB] + dot(u[TOPL : TOPL + RB, S:], fhi[...])
    own = both[RB:]
    part_mid = jnp.sum(cross * own, axis=0, keepdims=True) + jnp.sum(jnp.where(eye, dinv[...], 0.0), axis=0, keepdims=True)
    for r0, rl, val in ((TOP, TOPL, cross), (BOT, BOTL, own)):
        hi, lo = split(-val)
        u[r0 : r0 + RB, :S] = hi
        u[rl : rl + RB, :S] = lo
    for b in range(2):
        pick(0, ROWS, b)

    halves(1, xl)
    H = TOPL
    early = dot(v[:, :S], fhi[:S])
    low = dot(v[:H, :S], flo[:S])
    tall = dot(v[: 2 * RB, S:], fhi[S:]) + dot(v[: 2 * RB, S:], flo[S:])
    tail = dot(v[TOPL : TOPL + RB, S:], fhi[S:])
    front = early[:H] + low
    top = front[:RB] + early[TOPL : TOPL + RB] + tall[:RB] + tail
    bot = front[BOT : BOT + RB] + early[BOTL : BOTL + RB] + tall[RB:]
    kk = front[DI : DI + RK] + early[DIL : DIL + RK]
    part_low = jnp.sum(top * bot, axis=0, keepdims=True) + jnp.sum(kk * front[ID : ID + RK], axis=0, keepdims=True)

    for k in range(4):
        fin[tile, k : k + 1] = part_mid[:, k * 128 : (k + 1) * 128]
        fin[tile, k + 4 : k + 5] = part_low[:, k * 128 : (k + 1) * 128]
    for d in range(1, NT):
        send(fin.at[tile], fin.at[tile], f_send, f_recv, (leaf, lax.rem(tile + d, NT)))
    wait(fin.at[pl.ds(0, NT - 1)], f_recv)
    total = jnp.sum(fin[...], axis=0)
    per = 128 // RK
    row = lax.broadcasted_iota(jnp.int32, (8, 128), 0)
    turn = lax.rem(128 - lax.rem(tile, per) * RK, 128)
    for out, base, add in ((out_mid, 0, None), (out_low, 4, dlow)):
        line = jnp.sum(jnp.where(row == base + tile // per, total, 0.0), axis=0, keepdims=True)
        line = pltpu.roll(jnp.broadcast_to(line, (8, 128)), turn, 1)[0:1, :RK]
        out[...] = line if add is None else line + add[...]

    wait(fin.at[pl.ds(0, NT - 1)], f_send)
    wait(pmbuf.at[pl.ds(0, 3)], p_send)
    wait(ygath.at[pl.ds(0, NY - 1)], y_send)
    wait(stage, x_send)
    for a, (_, whole) in enumerate(facs):
        wait(whole.at[pl.ds(0, NZ - 1)], z_send.at[a])
        wait(whole.at[pl.ds(0, NZ)], c_send.at[a])


def body(parent_cov, parent_map, front_rows, rows_mid, rows_low, factor_mid, dinv_mid, factor_low, diag_low):
    vm, sm = pl.BlockSpec(memory_space=pltpu.VMEM), pl.BlockSpec(memory_space=pltpu.SMEM)
    dma = pltpu.SemaphoreType.DMA
    return pl.pallas_call(
        kernel,
        out_shape=[jax.ShapeDtypeStruct((1, RK), F32)] * 2,
        in_specs=[vm, sm, sm, vm, vm, vm, vm, vm, vm],
        out_specs=[vm, vm],
        scratch_shapes=[
            pltpu.VMEM((NY, 4, HB, 128), F32),
            pltpu.VMEM((NX - 1, NY, HB, 128), F32),
            pltpu.VMEM((NX * NY, HB, 128), F32),
            pltpu.VMEM((NX, 8, 128), jnp.int32),
            pltpu.VMEM((NT, RF, S), F32),
            pltpu.VMEM((NT, RF, S), F32),
            pltpu.VMEM((NB, WIN, BLK), BF),
            pltpu.VMEM((NB, WIN, BLK), BF),
            pltpu.VMEM((2 * RB, F), BF),
            pltpu.VMEM((ROWS, F), BF),
            pltpu.VMEM((ROWS, M), BF),
            pltpu.VMEM((M, S), BF),
            pltpu.VMEM((M, S), BF),
            pltpu.VMEM((NT, 8, 128), F32),
            dma, dma((2, 4)), dma, dma, dma, dma, dma((2,)), dma((2, 2, 4)), dma((2,)), dma((2,)), dma, dma, dma((2,)),
        ],
        compiler_params=pltpu.CompilerParams(
            collective_id=0, has_side_effects=True, vmem_limit_bytes=48 * 1024 * 1024
        ),
        cost_estimate=pl.CostEstimate(flops=5 * 10**9, bytes_accessed=10**6, transcendentals=0),
    )(parent_cov, parent_map, front_rows, rows_mid, rows_low, factor_mid[0], dinv_mid[0], factor_low[0], diag_low)


def solution(mesh):
    return jax.shard_map(
        body,
        mesh=mesh,
        in_specs=(
            P(None, "tile", "leaf"),
            P("leaf"),
            P("leaf", None),
            P("leaf", None),
            P("leaf", None),
            P("leaf", "tile", None),
            P("leaf", "tile", None),
            P("leaf", "tile", None),
            P("leaf", "tile"),
        ),
        out_specs=(P("leaf", "tile"), P("leaf", "tile")),
        check_vma=False,
    )
```

```python
import jax
import jax.numpy as jnp
from jax import lax
from jax.experimental import pallas as pl
from jax.experimental.pallas import tpu as pltpu
from jax.sharding import PartitionSpec as P

NX, NY, NZ, NC = 4, 8, 8, 2
NT, NL = NZ * NC, NX * NY
NP, S, M, F = 4, 512, 1536, 2048
RB = F // NT
RF = M // NT
RK = S // NT
CB = F // NL
PL = NC * RF
WIN, BLK = 768, 256
NB = M // BLK
BF, F32, I32 = jnp.bfloat16, jnp.float32, jnp.int32
MESH = pl.DeviceIdType.MESH
AHEAD = 9

TOP, BOT, DI, ID, TOPL, BOTL, DIL, ROWS = 0, RB, 2 * RB, 2 * RB + RK, 2 * RB + 2 * RK, 3 * RB + 2 * RK, 4 * RB + 2 * RK, 4 * RB + 3 * RK


def ring_order():
    def pieces(a, s):
        if s < 3:
            return [(a, s, 0, 32), (a, s, 32, 32), (a, s, 64, 32)]
        return [(a, s, 0, 32), (a, s, 32, 16)]

    up = []
    for s in range(5):
        up += (pieces(0, s) if s < 4 else []) + (pieces(1, s - 1) if s > 0 else [])
    down = [(a, s, RF - r - n, n) for a, s, r, n in up]
    return up, down


UP, DOWN = ring_order()
NPIECE = len(UP)


def source_of(seq, k):
    a, s, r, n = seq[k]
    return next(i for i, (b, q, r0, m) in enumerate(seq) if b == a and q == s - 1 and r0 <= r and r + n <= r0 + m)


def split(v):
    hi = v.astype(BF)
    return hi, (v - hi.astype(F32)).astype(BF)


def dot(a, b):
    return jnp.dot(a, b, preferred_element_type=F32)


def kernel(
    pmap, counts, cov, rows_mid, rows_low, fm, dinv, fl, dlow,
    out_mid, out_low,
    ygath, stage, covsel, pmbuf, xm, xl, rbuf, dbuf, lbuf, qoh, roh, csrc, u, v, fhi, flo, yhi, ylo, fin,
    y_send, y_recv, x_send, x_recv, p_send, p_recv, z_send, z_recv, c_send, c_recv, f_send, f_recv, l_sem,
):
    leaf, tile = lax.axis_index("leaf"), lax.axis_index("tile")
    x, y = leaf // NY, leaf % NY
    z, c = tile // NC, tile % NC

    def leaf_at(dx, dy):
        return lax.rem(x + dx + NX, NX) * NY + lax.rem(y + dy + NY, NY)

    def zt(dz):
        return lax.rem(z + dz + NZ, NZ) * NC + c

    sibling = z * NC + (1 - c)
    up, down = zt(1), zt(-1)
    ynext, yprev = leaf_at(0, 1), leaf_at(0, -1)
    own, whole = (fm, fl), (xm, xl)

    barrier = pltpu.get_barrier_semaphore()
    near = [(leaf, up), (leaf, down), (leaf, sibling), (ynext, tile), (yprev, tile)]
    near += [(leaf_at(dx, 0), tile) for dx in (1, 2, 3)]
    for other in near:
        pl.semaphore_signal(barrier, inc=1, device_id=other, device_id_type=MESH)

    local = [
        (cov, ygath.at[y]), (rows_mid, rbuf.at[0:1]), (rows_low, rbuf.at[1:2]), (dinv, dbuf), (dlow, lbuf),
        (fm, xm.at[tile]), (fl, xl.at[tile]),
    ]
    local = [pltpu.make_async_copy(src, dst, l_sem.at[i]) for i, (src, dst) in enumerate(local)]
    for copy in local:
        copy.start()
    pmbuf[x] = jnp.full((8, 128), pmap[0], I32)
    pl.semaphore_wait(barrier, len(near))

    def send(src, dst, ssem, rsem, where):
        pltpu.make_async_remote_copy(
            src_ref=src, dst_ref=dst, send_sem=ssem, recv_sem=rsem, device_id=where, device_id_type=MESH
        ).start()

    def wait(ref, sem):
        pltpu.make_async_copy(ref, ref, sem).wait()

    def y_piece(d, j):
        s, p = divmod(j, NP)
        return s, (p if d == 0 else NP - 1 - p)

    def y_go(d, j):
        s, p = y_piece(d, j)
        src_y = lax.rem(y + (NY - s if d == 0 else s), NY)
        dst = ygath.at[src_y, p]
        send(cov.at[p] if s == 0 else dst, dst, y_send, y_recv.at[d, j], (ynext if d == 0 else yprev, tile))

    def y_come(d, j):
        s, p = y_piece(d, j)
        wait(ygath.at[lax.rem(y + (NY - 1 - s if d == 0 else s + 1), NY), p], y_recv.at[d, j])

    def z_go(d, k):
        a, s, r, n = (UP, DOWN)[d][k]
        dst = whole[a].at[zt(-s if d == 0 else s), pl.ds(r, n)]
        send(own[a].at[pl.ds(r, n)] if s == 0 else dst, dst, z_send, z_recv.at[d, k], (leaf, up if d == 0 else down))

    def z_come(d, k):
        a, s, r, n = (UP, DOWN)[d][k]
        wait(whole[a].at[zt(-s - 1 if d == 0 else s + 1), pl.ds(r, n)], z_recv.at[d, k])

    for dx in (1, 2, 3):
        send(pmbuf.at[x], pmbuf.at[x], p_send, p_recv, (leaf_at(dx, 0), tile))
    for j in range(NP):
        y_go(0, j)
        y_go(1, j)
    due = {}
    for d, seq in ((0, UP), (1, DOWN)):
        for k in range(NPIECE):
            after = k - AHEAD if seq[k][1] == 0 else max(k - AHEAD, source_of(seq, k))
            if after < 0:
                z_go(d, k)
            else:
                due.setdefault(after, []).append((d, k))
    for a in range(2):
        send(own[a], whole[a].at[tile], c_send, c_recv.at[a, 0], (leaf, sibling))

    for copy in local:
        copy.wait()
    live_mid, live_low = counts[0, 0], counts[0, 1]
    lane = lax.broadcasted_iota(I32, (1, M), 1)
    midv = jnp.where(lane < live_mid, rbuf[0:1], -1)
    lowv = jnp.where(lane < live_low, rbuf[1:2], -1)
    eye = lax.broadcasted_iota(I32, (RK, S), 0) + tile * RK == lax.broadcasted_iota(I32, (RK, S), 1)

    def mid_onehot(b):
        pos = lax.broadcasted_iota(I32, (WIN, BLK), 0) + b * BLK
        qoh[b] = (pos == midv[:, b * BLK : (b + 1) * BLK]).astype(F32).astype(BF)

    def low_start(p):
        return p * PL // 128 * 128

    def low_onehot(p):
        pos = lax.broadcasted_iota(I32, (WIN, PL), 0) + low_start(p)
        roh[p] = (pos == lowv[:, p * PL : (p + 1) * PL]).astype(F32).astype(BF)

    def rows_without_transfer():
        u[BOT : BOT + RB, S:] = (lax.broadcasted_iota(I32, (RB, M), 0) + tile * RB == midv).astype(F32).astype(BF)
        dhi, dlo = split(dbuf[...])
        u[DI : DI + RK, :S] = dhi
        u[ID : ID + RK, :S] = eye.astype(F32).astype(BF)
        u[DIL : DIL + RK, :S] = dlo
        for r0, n in ((DI, 2 * RK), (BOTL, RB + RK)):
            u[r0 : r0 + n, S:] = jnp.zeros((n, M), BF)

    def choose(ys):
        for dx in range(NX):
            pm = jnp.broadcast_to(pmbuf[lax.rem(x + dx, NX)][0:1], (CB, RB))
            got = jnp.where(
                pm < 2,
                jnp.where(pm == 0, ygath[ys, 0], ygath[ys, 1]),
                jnp.where(pm == 2, ygath[ys, 2], ygath[ys, 3]),
            )
            if dx == 0:
                covsel[x * NY + ys] = got
            else:
                stage[dx - 1, ys] = got
                send(stage.at[dx - 1, ys], covsel.at[x * NY + ys], x_send, x_recv, (leaf_at(dx, 0), tile))

    def pass_on(a, s):
        for t in (zt(-s), zt(s))[: 2 if s < 4 else 1]:
            send(whole[a].at[t], whole[a].at[t], c_send, c_recv.at[a, s], (leaf, sibling))

    def parent_columns():
        wait(covsel.at[pl.ds(0, (NX - 1) * NY)], x_recv)
        for m in range(F // 128):
            hi, lo = split(covsel[2 * m : 2 * m + 2].reshape(128, RB).T)
            csrc[:RB, m * 128 : (m + 1) * 128] = hi
            csrc[RB:, m * 128 : (m + 1) * 128] = lo
        for b in range(NB):
            got = dot(csrc[:, b * BLK : b * BLK + WIN], qoh[b]).astype(BF)
            u[TOP : TOP + RB, S + b * BLK : S + (b + 1) * BLK] = got[:RB]
            u[TOPL : TOPL + RB, S + b * BLK : S + (b + 1) * BLK] = got[RB:]

    def pick(p):
        v[p] = dot(u[:, low_start(p) : low_start(p) + WIN], roh[p]).astype(BF)

    def chip_rows(a, s):
        return (z,) if s == 0 else (lax.rem(z + s, NZ),) if s == 4 else (lax.rem(z + NZ - s, NZ), lax.rem(z + s, NZ))

    def come_from_sibling(a, s):
        wait(whole[a].at[pl.ds(0, 2 if 0 < s < 4 else 1)], c_recv.at[a, s])

    def mid_halves(s):
        come_from_sibling(0, s)
        for p in chip_rows(0, s):
            hi, lo = split(xm[pl.ds(p * NC, NC)].reshape(PL, S))
            fhi[pl.ds(p * PL, PL)] = hi
            flo[pl.ds(p * PL, PL)] = lo

    def low_terms(s):
        come_from_sibling(1, s)
        for p in chip_rows(1, s):
            hi, lo = split(xl[pl.ds(p * NC, NC)].reshape(PL, S))
            left = v[p]
            first, second = dot(left, hi), dot(left[:TOPL], lo)
            yhi[...] = first if s == 0 else yhi[...] + first
            ylo[...] = second if s == 0 else ylo[...] + second

    def cross_rows():
        both = dot(u[: 2 * RB, S:], fhi[...]) + dot(u[: 2 * RB, S:], flo[...])
        cross = both[:RB] + dot(u[TOPL : TOPL + RB, S:], fhi[...])
        mine = both[RB:]
        part = jnp.sum(cross * mine, axis=0, keepdims=True) + jnp.sum(jnp.where(eye, dbuf[...], 0.0), axis=0, keepdims=True)
        for k in range(4):
            fin[tile, k : k + 1] = part[:, k * 128 : (k + 1) * 128]
        for r0, rl, val in ((TOP, TOPL, cross), (BOT, BOTL, mine)):
            hi, lo = split(-val)
            u[r0 : r0 + RB, :S] = hi
            u[rl : rl + RB, :S] = lo

    rows_without_transfer()
    wait(pmbuf.at[pl.ds(0, 3)], p_recv)
    choose(y)

    beside = {}

    def at(k, f, *args):
        beside.setdefault(k, []).append((f, args))

    for b in range(NB):
        at(3 + b, mid_onehot, b)
    for p in range(NZ):
        at(4 + p, low_onehot, p)
    at(8, mid_halves, 0)
    at(9, mid_halves, 1)
    at(10, mid_halves, 2)
    at(12, parent_columns)
    for p in range(3, NZ):
        at(13, pick, p)
    at(14, mid_halves, 3)
    at(17, mid_halves, 4)
    at(17, cross_rows)
    for p in range(3):
        at(17, pick, p)
    for s in range(3):
        at(18, low_terms, s)
    at(19, low_terms, 3)
    at(21, low_terms, 4)

    ny = 3 * NP + NP // 2
    jy = 0
    for k in range(NPIECE):
        while jy < ny and jy <= 2 * k:
            for d in (0, 1):
                y_come(d, jy)
                if jy + NP < ny:
                    y_go(d, jy + NP)
            s, p = divmod(jy, NP)
            if s < 3 and p == NP - 1:
                choose(lax.rem(y + NY - 1 - s, NY))
                choose(lax.rem(y + s + 1, NY))
            elif jy == ny - 1:
                choose(lax.rem(y + NY // 2, NY))
            jy += 1
        z_come(0, k)
        z_come(1, k)
        for d, q in due.get(k, ()):
            z_go(d, q)
        a, s = UP[k][:2]
        if k + 1 == NPIECE or UP[k + 1][:2] != (a, s):
            pass_on(a, s + 1)
        for f, args in beside.get(k, ()):
            f(*args)

    def rows(r0, rl, n):
        return yhi[r0 : r0 + n] + yhi[rl : rl + n] + ylo[r0 : r0 + n]

    part = jnp.sum(rows(TOP, TOPL, RB) * rows(BOT, BOTL, RB), axis=0, keepdims=True)
    part += jnp.sum(rows(DI, DIL, RK) * (yhi[ID : ID + RK] + ylo[ID : ID + RK]), axis=0, keepdims=True)
    for k in range(4):
        fin[tile, k + 4 : k + 5] = part[:, k * 128 : (k + 1) * 128]

    for d in sorted(range(1, NT), key=lambda d: -min(d, NT - d)):
        send(fin.at[tile], fin.at[tile], f_send, f_recv, (leaf, lax.rem(tile + d, NT)))
    wait(fin.at[pl.ds(0, NT - 1)], f_recv)
    total = jnp.sum(fin[...], axis=0)
    per = 128 // RK
    row = lax.broadcasted_iota(I32, (8, 128), 0)
    turn = lax.rem(128 - lax.rem(tile, per) * RK, 128)
    for out, base, add in ((out_mid, 0, None), (out_low, 4, lbuf)):
        line = jnp.sum(jnp.where(row == base + tile // per, total, 0.0), axis=0, keepdims=True)
        line = pltpu.roll(jnp.broadcast_to(line, (8, 128)), turn, 1)[0:1, :RK]
        out[...] = line if add is None else line + add[...]

    wait(fin.at[pl.ds(0, NT - 1)], f_send)
    wait(pmbuf.at[pl.ds(0, 3)], p_send)
    wait(ygath.at[pl.ds(0, NY - 1)], y_send)
    wait(stage, x_send)
    for w in whole:
        wait(w.at[pl.ds(0, NZ - 1)], z_send)
        wait(w.at[pl.ds(0, NZ)], c_send)


def body(parent_cov, parent_map, front_rows, rows_mid, rows_low, factor_mid, dinv_mid, factor_low, diag_low):
    vm, sm, hb = (pl.BlockSpec(memory_space=s) for s in (pltpu.VMEM, pltpu.SMEM, pl.ANY))
    dma = pltpu.SemaphoreType.DMA
    return pl.pallas_call(
        kernel,
        out_shape=[jax.ShapeDtypeStruct((1, RK), F32)] * 2,
        in_specs=[sm, sm] + [hb] * 7,
        out_specs=[vm, vm],
        scratch_shapes=[
            pltpu.VMEM((NY, NP, CB, RB), F32),
            pltpu.VMEM((NX - 1, NY, CB, RB), F32),
            pltpu.VMEM((NL, CB, RB), F32),
            pltpu.VMEM((NX, 8, 128), I32),
            pltpu.VMEM((NT, RF, S), F32),
            pltpu.VMEM((NT, RF, S), F32),
            pltpu.VMEM((2, M), I32),
            pltpu.VMEM((RK, S), F32),
            pltpu.VMEM((1, RK), F32),
            pltpu.VMEM((NB, WIN, BLK), BF),
            pltpu.VMEM((NZ, WIN, PL), BF),
            pltpu.VMEM((2 * RB, F), BF),
            pltpu.VMEM((ROWS, F), BF),
            pltpu.VMEM((NZ, ROWS, PL), BF),
            pltpu.VMEM((M, S), BF),
            pltpu.VMEM((M, S), BF),
            pltpu.VMEM((ROWS, S), F32),
            pltpu.VMEM((TOPL, S), F32),
            pltpu.VMEM((NT, 8, 128), F32),
            dma, dma((2, 14)), dma, dma, dma, dma, dma, dma((2, NPIECE)), dma, dma((2, 5)), dma, dma, dma((7,)),
        ],
        compiler_params=pltpu.CompilerParams(
            collective_id=0, has_side_effects=True, vmem_limit_bytes=60 * 1024 * 1024
        ),
        cost_estimate=pl.CostEstimate(flops=5 * 10**9, bytes_accessed=10**6, transcendentals=0),
    )(
        parent_map, front_rows, jnp.swapaxes(parent_cov, 1, 2), rows_mid, rows_low,
        factor_mid[0], dinv_mid[0], factor_low[0], diag_low,
    )


def solution(mesh):
    return jax.shard_map(
        body,
        mesh=mesh,
        in_specs=(
            P(None, "tile", "leaf"),
            P("leaf"),
            P("leaf", None),
            P("leaf", None),
            P("leaf", None),
            P("leaf", "tile", None),
            P("leaf", "tile", None),
            P("leaf", "tile", None),
            P("leaf", "tile"),
        ),
        out_specs=(P("leaf", "tile"), P("leaf", "tile")),
        check_vma=False,
    )
```

```python
import jax
import jax.numpy as jnp
from jax import lax
from jax.experimental import pallas as pl
from jax.experimental.pallas import tpu as pltpu
from jax.sharding import PartitionSpec as P

NX, NY, NZ, NC = 4, 8, 8, 2
NT, NL = NZ * NC, NX * NY
NP, S, M, F = 4, 512, 1536, 2048
RB = F // NT
RF = M // NT
RK = S // NT
CB = F // NL
PL = NC * RF
WIN, BLK = 768, 256
NB = M // BLK
BF, F32, I32 = jnp.bfloat16, jnp.float32, jnp.int32
MESH = pl.DeviceIdType.MESH
AHEAD, LAG = 4, 1

TOP, BOT, DI, ID, TOPL, BOTL, DIL, ROWS = 0, RB, 2 * RB, 2 * RB + RK, 2 * RB + 2 * RK, 3 * RB + 2 * RK, 4 * RB + 2 * RK, 4 * RB + 3 * RK


def ring_order():
    def pieces(a, s):
        if s < 3:
            return [(a, s, 0, 48), (a, s, 48, 48)]
        return [(a, s, 0, 48)]

    up = []
    for s in range(4 + LAG):
        up += (pieces(0, s) if s < 4 else []) + (pieces(1, s - LAG) if s >= LAG else [])
    down = [(a, s, RF - r - n, n) for a, s, r, n in up]
    return up, down


UP, DOWN = ring_order()
NPIECE = len(UP)


def source_of(seq, k):
    a, s, r, n = seq[k]
    return next(i for i, (b, q, r0, m) in enumerate(seq) if b == a and q == s - 1 and r0 <= r and r + n <= r0 + m)


def split(v):
    hi = v.astype(BF)
    return hi, (v - hi.astype(F32)).astype(BF)


def dot(a, b):
    return jnp.dot(a, b, preferred_element_type=F32)


def kernel(
    pmap_hbm, counts_hbm, cov, rows_mid, rows_low, fm, dinv, fl, dlow,
    out,
    ygath, stage, covsel, pmbuf, xm, xl, rbuf, dbuf, lbuf, qoh, roh, csrc, u, v, fhi, flo, yhi, ylo, fin, pmap, counts,
    y_send, y_recv, x_send, x_recv, p_send, p_recv, z_send, z_recv, c_send, c_recv, f_send, f_recv, l_sem,
):
    leaf, tile = lax.axis_index("leaf"), lax.axis_index("tile")
    x, y = leaf // NY, leaf % NY
    z, c = tile // NC, tile % NC

    def leaf_at(dx, dy):
        return lax.rem(x + dx + NX, NX) * NY + lax.rem(y + dy + NY, NY)

    def zt(dz):
        return lax.rem(z + dz + NZ, NZ) * NC + c

    sibling = z * NC + (1 - c)
    up, down = zt(1), zt(-1)
    ynext, yprev = leaf_at(0, 1), leaf_at(0, -1)
    own, whole = (fm, fl), (xm, xl)

    barrier = pltpu.get_barrier_semaphore()
    near = [(leaf, up), (leaf, down), (leaf, sibling), (ynext, tile), (yprev, tile)]
    near += [(leaf_at(dx, 0), tile) for dx in (1, 2, 3)]
    for other in near:
        pl.semaphore_signal(barrier, inc=1, device_id=other, device_id_type=MESH)

    parent = pltpu.make_async_copy(pmap_hbm, pmap, l_sem.at[8])
    parent.start()
    local = [
        (cov, ygath.at[y]), (rows_mid, rbuf.at[0:1]), (rows_low, rbuf.at[1:2]), (dinv, dbuf), (dlow, lbuf),
        (counts_hbm, counts), (fm, xm.at[tile]), (fl, xl.at[tile]),
    ]
    local = [pltpu.make_async_copy(src, dst, l_sem.at[i]) for i, (src, dst) in enumerate(local)]
    for copy in local:
        copy.start()
    pl.semaphore_wait(barrier, len(near))

    def send(src, dst, ssem, rsem, where):
        pltpu.make_async_remote_copy(
            src_ref=src, dst_ref=dst, send_sem=ssem, recv_sem=rsem, device_id=where, device_id_type=MESH
        ).start()

    def wait(ref, sem):
        pltpu.make_async_copy(ref, ref, sem).wait()

    def y_piece(d, j):
        s, p = divmod(j, 2)
        return s, pl.ds(2 * (p if d == 0 else 1 - p), 2)

    def y_go(d, j):
        s, p = y_piece(d, j)
        src_y = lax.rem(y + (NY - s if d == 0 else s), NY)
        dst = ygath.at[src_y, p]
        send(cov.at[p] if s == 0 else dst, dst, y_send, y_recv.at[d, j], (ynext if d == 0 else yprev, tile))

    def y_come(d, j):
        s, p = y_piece(d, j)
        wait(ygath.at[lax.rem(y + (NY - 1 - s if d == 0 else s + 1), NY), p], y_recv.at[d, j])

    def z_go(d, k):
        a, s, r, n = (UP, DOWN)[d][k]
        dst = whole[a].at[zt(-s if d == 0 else s), pl.ds(r, n)]
        send(own[a].at[pl.ds(r, n)] if s == 0 else dst, dst, z_send, z_recv.at[d, k], (leaf, up if d == 0 else down))

    def z_come(d, k):
        a, s, r, n = (UP, DOWN)[d][k]
        wait(whole[a].at[zt(-s - 1 if d == 0 else s + 1), pl.ds(r, n)], z_recv.at[d, k])

    parent.wait()
    pmbuf[x] = jnp.full((8, 128), pmap[0], I32)
    for dx in (1, 2, 3):
        send(pmbuf.at[x], pmbuf.at[x], p_send, p_recv, (leaf_at(dx, 0), tile))
    due = ({}, {})
    for d, seq in ((0, UP), (1, DOWN)):
        for k in range(NPIECE):
            after = k - AHEAD if seq[k][1] == 0 else max(k - AHEAD, source_of(seq, k))
            if after < 0:
                z_go(d, k)
            else:
                due[d].setdefault(after, []).append(k)
    for j in range(2):
        y_go(0, j)
        y_go(1, j)
    for a in range(2):
        send(own[a], whole[a].at[tile], c_send, c_recv.at[a, 0], (leaf, sibling))

    for copy in local:
        copy.wait()
    live_mid, live_low = counts[0, 0], counts[0, 1]
    lane = lax.broadcasted_iota(I32, (1, M), 1)
    midv = jnp.where(lane < live_mid, rbuf[0:1], -1)
    lowv = jnp.where(lane < live_low, rbuf[1:2], -1)
    eye = lax.broadcasted_iota(I32, (RK, S), 0) + tile * RK == lax.broadcasted_iota(I32, (RK, S), 1)

    def mid_onehot(b):
        pos = lax.broadcasted_iota(I32, (WIN, BLK), 0) + b * BLK
        qoh[b] = (pos == midv[:, b * BLK : (b + 1) * BLK]).astype(F32).astype(BF)

    def low_start(p):
        return p * PL // 128 * 128

    def low_onehot(p):
        pos = lax.broadcasted_iota(I32, (WIN, PL), 0) + low_start(p)
        roh[p] = (pos == lowv[:, p * PL : (p + 1) * PL]).astype(F32).astype(BF)

    def rows_without_transfer():
        u[BOT : BOT + RB, S:] = (lax.broadcasted_iota(I32, (RB, M), 0) + tile * RB == midv).astype(F32).astype(BF)
        dhi, dlo = split(dbuf[...])
        u[DI : DI + RK, :S] = dhi
        u[ID : ID + RK, :S] = eye.astype(F32).astype(BF)
        u[DIL : DIL + RK, :S] = dlo
        for r0, n in ((DI, 2 * RK), (BOTL, RB + RK)):
            u[r0 : r0 + n, S:] = jnp.zeros((n, M), BF)

    def choose(ys):
        for dx in range(NX):
            pm = jnp.broadcast_to(pmbuf[lax.rem(x + dx, NX)][0:1], (CB, RB))
            got = jnp.where(
                pm < 2,
                jnp.where(pm == 0, ygath[ys, 0], ygath[ys, 1]),
                jnp.where(pm == 2, ygath[ys, 2], ygath[ys, 3]),
            )
            if dx == 0:
                covsel[x * NY + ys] = got
            else:
                stage[dx - 1, ys] = got
                send(stage.at[dx - 1, ys], covsel.at[x * NY + ys], x_send, x_recv, (leaf_at(dx, 0), tile))

    def pass_on(a, s):
        for t in (zt(-s), zt(s)):
            send(whole[a].at[t], whole[a].at[t], c_send, c_recv.at[a, s], (leaf, sibling))

    def parent_columns():
        wait(covsel.at[pl.ds(0, (NX - 1) * NY)], x_recv)
        for m in range(F // 128):
            hi, lo = split(covsel[2 * m : 2 * m + 2].reshape(128, RB).T)
            csrc[:RB, m * 128 : (m + 1) * 128] = hi
            csrc[RB:, m * 128 : (m + 1) * 128] = lo
        for b in range(NB):
            got = dot(csrc[:, b * BLK : b * BLK + WIN], qoh[b]).astype(BF)
            u[TOP : TOP + RB, S + b * BLK : S + (b + 1) * BLK] = got[:RB]
            u[TOPL : TOPL + RB, S + b * BLK : S + (b + 1) * BLK] = got[RB:]

    def pick(p):
        v[p] = dot(u[:, low_start(p) : low_start(p) + WIN], roh[p]).astype(BF)

    def chip_rows(a, s):
        return (z,) if s == 0 else (lax.rem(z + s, NZ),) if s == 4 else (lax.rem(z + NZ - s, NZ), lax.rem(z + s, NZ))

    def come_from_sibling(a, s):
        wait(whole[a].at[pl.ds(0, 2 if 0 < s < 4 else 1)], c_recv.at[a, s])

    def mid_halves(s):
        come_from_sibling(0, s)
        for p in chip_rows(0, s):
            hi, lo = split(xm[pl.ds(p * NC, NC)].reshape(PL, S))
            fhi[pl.ds(p * PL, PL)] = hi
            flo[pl.ds(p * PL, PL)] = lo

    def low_terms(s):
        come_from_sibling(1, s)
        for p in chip_rows(1, s):
            hi, lo = split(xl[pl.ds(p * NC, NC)].reshape(PL, S))
            left = v[p]
            first, second = dot(left, hi), dot(left[:TOPL], lo)
            yhi[...] = first if s == 0 else yhi[...] + first
            ylo[...] = second if s == 0 else ylo[...] + second

    def cross_rows():
        both = dot(u[: 2 * RB, S:], fhi[...]) + dot(u[: 2 * RB, S:], flo[...])
        cross = both[:RB] + dot(u[TOPL : TOPL + RB, S:], fhi[...])
        mine = both[RB:]
        part = jnp.sum(cross * mine, axis=0, keepdims=True) + jnp.sum(jnp.where(eye, dbuf[...], 0.0), axis=0, keepdims=True)
        for k in range(4):
            fin[tile, k : k + 1] = part[:, k * 128 : (k + 1) * 128]
        for r0, rl, val in ((TOP, TOPL, cross), (BOT, BOTL, mine)):
            hi, lo = split(-val)
            u[r0 : r0 + RB, :S] = hi
            u[rl : rl + RB, :S] = lo

    rows_without_transfer()
    wait(pmbuf.at[pl.ds(0, 3)], p_recv)
    choose(y)

    todo = [[] for _ in range(NPIECE)]

    def at(k, f, *args):
        todo[k].append((f, args))

    for b in range(NB):
        at(b // 3, mid_onehot, b)
    for p in range(NZ):
        at(2 + p // 4, low_onehot, p)
    at(4, mid_halves, 0)
    at(5, mid_halves, 1)
    at(7, mid_halves, 2)
    at(8, parent_columns)
    for p in range(3, NZ):
        at(9, pick, p)
    at(9, mid_halves, 3)
    at(10, mid_halves, 4)
    at(10, cross_rows)
    for p in range(3):
        at(11, pick, p)
    at(11, low_terms, 0)
    at(12, low_terms, 1)
    at(12, low_terms, 2)
    at(13, low_terms, 3)
    at(13, low_terms, 4)

    ny = 7
    jy = 0
    for k in range(NPIECE):
        while jy < ny and jy <= k:
            for d in (0, 1):
                y_come(d, jy)
                if jy + 2 < ny:
                    y_go(d, jy + 2)
            s, p = divmod(jy, 2)
            if s < 3 and p == 1:
                choose(lax.rem(y + NY - 1 - s, NY))
                choose(lax.rem(y + s + 1, NY))
            elif jy == ny - 1:
                choose(lax.rem(y + NY // 2, NY))
            jy += 1
        a, s = UP[k][:2]
        for d in (0, 1):
            z_come(d, k)
            for q in due[d].get(k, ()):
                z_go(d, q)
            if s == 3:
                half = whole[a].at[zt(4), pl.ds((UP, DOWN)[d][k][2], RF // 2)]
                send(half, half, c_send, c_recv.at[a, 4], (leaf, sibling))
        if s < 3 and UP[k + 1][:2] != (a, s):
            pass_on(a, s + 1)
        for f, args in todo[k]:
            f(*args)

    def rows(r0, rl, n):
        return yhi[r0 : r0 + n] + yhi[rl : rl + n] + ylo[r0 : r0 + n]

    part = jnp.sum(rows(TOP, TOPL, RB) * rows(BOT, BOTL, RB), axis=0, keepdims=True)
    part += jnp.sum(rows(DI, DIL, RK) * (yhi[ID : ID + RK] + ylo[ID : ID + RK]), axis=0, keepdims=True)
    for k in range(4):
        fin[tile, k + 4 : k + 5] = part[:, k * 128 : (k + 1) * 128]

    for d in sorted(range(1, NT), key=lambda d: -min(d, NT - d)):
        send(fin.at[tile], fin.at[tile], f_send, f_recv, (leaf, lax.rem(tile + d, NT)))
    wait(fin.at[pl.ds(0, NT - 1)], f_recv)
    total = jnp.sum(fin[...], axis=0)
    per = 128 // RK
    row = lax.broadcasted_iota(I32, (8, 128), 0)
    turn = lax.rem(128 - lax.rem(tile, per) * RK, 128)
    for o, base, add in ((0, 0, None), (1, 4, lbuf)):
        line = jnp.sum(jnp.where(row == base + tile // per, total, 0.0), axis=0, keepdims=True)
        line = pltpu.roll(jnp.broadcast_to(line, (8, 128)), turn, 1)[0:1, :RK]
        out[o : o + 1] = line if add is None else line + add[...]

    wait(fin.at[pl.ds(0, NT - 1)], f_send)
    wait(pmbuf.at[pl.ds(0, 3)], p_send)
    wait(ygath.at[pl.ds(0, NY - 1)], y_send)
    wait(stage, x_send)
    for w in whole:
        wait(w.at[pl.ds(0, NZ - 1)], z_send)
        wait(w.at[pl.ds(0, NZ)], c_send)


def body(parent_cov, parent_map, front_rows, rows_mid, rows_low, factor_mid, dinv_mid, factor_low, diag_low):
    vm, hb = (pl.BlockSpec(memory_space=s) for s in (pltpu.VMEM, pl.ANY))
    dma = pltpu.SemaphoreType.DMA
    out = pl.pallas_call(
        kernel,
        out_shape=jax.ShapeDtypeStruct((2, RK), F32),
        in_specs=[hb] * 9,
        out_specs=vm,
        scratch_shapes=[
            pltpu.VMEM((NY, NP, CB, RB), F32),
            pltpu.VMEM((NX - 1, NY, CB, RB), F32),
            pltpu.VMEM((NL, CB, RB), F32),
            pltpu.VMEM((NX, 8, 128), I32),
            pltpu.VMEM((NT, RF, S), F32),
            pltpu.VMEM((NT, RF, S), F32),
            pltpu.VMEM((2, M), I32),
            pltpu.VMEM((RK, S), F32),
            pltpu.VMEM((1, RK), F32),
            pltpu.VMEM((NB, WIN, BLK), BF),
            pltpu.VMEM((NZ, WIN, PL), BF),
            pltpu.VMEM((2 * RB, F), BF),
            pltpu.VMEM((ROWS, F), BF),
            pltpu.VMEM((NZ, ROWS, PL), BF),
            pltpu.VMEM((M, S), BF),
            pltpu.VMEM((M, S), BF),
            pltpu.VMEM((ROWS, S), F32),
            pltpu.VMEM((TOPL, S), F32),
            pltpu.VMEM((NT, 8, 128), F32),
            pltpu.SMEM((1,), I32),
            pltpu.SMEM((1, 2), I32),
            dma, dma((2, 14)), dma, dma, dma, dma, dma, dma((2, NPIECE)), dma, dma((2, 5)), dma, dma, dma((9,)),
        ],
        compiler_params=pltpu.CompilerParams(
            collective_id=0, has_side_effects=True, vmem_limit_bytes=60 * 1024 * 1024
        ),
        cost_estimate=pl.CostEstimate(flops=5 * 10**9, bytes_accessed=10**6, transcendentals=0),
    )(
        parent_map, front_rows, jnp.swapaxes(parent_cov, 1, 2), rows_mid, rows_low,
        factor_mid[0], dinv_mid[0], factor_low[0], diag_low,
    )
    return out[0:1], out[1:2]


def solution(mesh):
    return jax.shard_map(
        body,
        mesh=mesh,
        in_specs=(
            P(None, "tile", "leaf"),
            P("leaf"),
            P("leaf", None),
            P("leaf", None),
            P("leaf", None),
            P("leaf", "tile", None),
            P("leaf", "tile", None),
            P("leaf", "tile", None),
            P("leaf", "tile"),
        ),
        out_specs=(P("leaf", "tile"), P("leaf", "tile")),
        check_vma=False,
    )
```

```python
import jax
import jax.numpy as jnp
from jax import lax
from jax.experimental import pallas as pl
from jax.experimental.pallas import tpu as pltpu
from jax.sharding import PartitionSpec as P

NX, NY, NZ, NC = 4, 8, 8, 2
NT, NL = NZ * NC, NX * NY
NP, S, M, F = 4, 512, 1536, 2048
RB = F // NT
RF = M // NT
RK = S // NT
CB = F // NL
PL = NC * RF
WIN, BLK = 768, 256
NB = M // BLK
BF, F32, I32 = jnp.bfloat16, jnp.float32, jnp.int32
MESH = pl.DeviceIdType.MESH
AHEAD, LAG = 4, 1

TOP, BOT, DI, ID, TOPL, BOTL, DIL, ROWS = 0, RB, 2 * RB, 2 * RB + RK, 2 * RB + 2 * RK, 3 * RB + 2 * RK, 4 * RB + 2 * RK, 4 * RB + 3 * RK


def ring_order():
    def pieces(a, s):
        if s < 3:
            return [(a, s, 0, 48), (a, s, 48, 48)]
        return [(a, s, 0, 48)]

    up = []
    for s in range(4 + LAG):
        up += (pieces(0, s) if s < 4 else []) + (pieces(1, s - LAG) if s >= LAG else [])
    down = [(a, s, RF - r - n, n) for a, s, r, n in up]
    return up, down


UP, DOWN = ring_order()
NPIECE = len(UP)


def source_of(seq, k):
    a, s, r, n = seq[k]
    return next(i for i, (b, q, r0, m) in enumerate(seq) if b == a and q == s - 1 and r0 <= r and r + n <= r0 + m)


def split(v):
    hi = v.astype(BF)
    return hi, (v - hi.astype(F32)).astype(BF)


def dot(a, b):
    return jnp.dot(a, b, preferred_element_type=F32)


def kernel(
    pmap_hbm, counts_hbm, cov, rows_mid, rows_low, fm, dinv, fl, dlow,
    out,
    ygath, stage, covsel, pmbuf, xm, xl, rbuf, dbuf, lbuf, qoh, roh, csrc, u, v, fhi, flo, yhi, ylo, fin, pmap, counts,
    y_send, y_recv, x_send, x_recv, p_send, p_recv, z_send, z_recv, c_send, c_recv, f_send, f_recv, l_sem,
):
    leaf, tile = lax.axis_index("leaf"), lax.axis_index("tile")
    x, y = leaf // NY, leaf % NY
    z, c = tile // NC, tile % NC

    def leaf_at(dx, dy):
        return lax.rem(x + dx + NX, NX) * NY + lax.rem(y + dy + NY, NY)

    def zt(dz):
        return lax.rem(z + dz + NZ, NZ) * NC + c

    sibling = z * NC + (1 - c)
    up, down = zt(1), zt(-1)
    ynext, yprev = leaf_at(0, 1), leaf_at(0, -1)
    own, whole = (fm, fl), (xm, xl)

    barrier = pltpu.get_barrier_semaphore()
    near = [(leaf, up), (leaf, down), (leaf, sibling), (ynext, tile), (yprev, tile)]
    near += [(leaf_at(dx, 0), tile) for dx in (1, 2, 3)]
    for other in near:
        pl.semaphore_signal(barrier, inc=1, device_id=other, device_id_type=MESH)

    parent = pltpu.make_async_copy(pmap_hbm, pmap, l_sem.at[8])
    parent.start()
    local = [
        (cov, ygath.at[y]), (rows_mid, rbuf.at[0:1]), (rows_low, rbuf.at[1:2]), (dinv, dbuf), (dlow, lbuf),
        (counts_hbm, counts), (fm, xm.at[tile]), (fl, xl.at[tile]),
    ]
    local = [pltpu.make_async_copy(src, dst, l_sem.at[i]) for i, (src, dst) in enumerate(local)]
    pl.semaphore_wait(barrier, len(near))

    def send(src, dst, ssem, rsem, where):
        pltpu.make_async_remote_copy(
            src_ref=src, dst_ref=dst, send_sem=ssem, recv_sem=rsem, device_id=where, device_id_type=MESH
        ).start()

    def wait(ref, sem):
        pltpu.make_async_copy(ref, ref, sem).wait()

    def y_piece(d, j):
        s, p = divmod(j, 2)
        return s, pl.ds(2 * (p if d == 0 else 1 - p), 2)

    def y_go(d, j):
        s, p = y_piece(d, j)
        src_y = lax.rem(y + (NY - s if d == 0 else s), NY)
        dst = ygath.at[src_y, p]
        send(cov.at[p] if s == 0 else dst, dst, y_send, y_recv.at[d, j], (ynext if d == 0 else yprev, tile))

    def y_come(d, j):
        s, p = y_piece(d, j)
        wait(ygath.at[lax.rem(y + (NY - 1 - s if d == 0 else s + 1), NY), p], y_recv.at[d, j])

    def z_go(d, k):
        a, s, r, n = (UP, DOWN)[d][k]
        dst = whole[a].at[zt(-s if d == 0 else s), pl.ds(r, n)]
        send(own[a].at[pl.ds(r, n)] if s == 0 else dst, dst, z_send, z_recv.at[d, k], (leaf, up if d == 0 else down))

    def z_come(d, k):
        a, s, r, n = (UP, DOWN)[d][k]
        wait(whole[a].at[zt(-s - 1 if d == 0 else s + 1), pl.ds(r, n)], z_recv.at[d, k])

    due = ({}, {})
    for k in range(NPIECE):
        for d, seq in ((0, UP), (1, DOWN)):
            after = k - AHEAD if seq[k][1] == 0 else max(k - AHEAD, source_of(seq, k))
            if after < 0:
                z_go(d, k)
            else:
                due[d].setdefault(after, []).append(k)
    for j in range(2):
        y_go(0, j)
        y_go(1, j)
    parent.wait()
    pmbuf[x] = jnp.full((8, 128), pmap[0], I32)
    for dx in (1, 2, 3):
        send(pmbuf.at[x], pmbuf.at[x], p_send, p_recv, (leaf_at(dx, 0), tile))
    for copy in local:
        copy.start()
    for a in range(2):
        send(own[a], whole[a].at[tile], c_send, c_recv.at[a, 0], (leaf, sibling))

    for copy in local:
        copy.wait()
    live_mid, live_low = counts[0, 0], counts[0, 1]
    lane = lax.broadcasted_iota(I32, (1, M), 1)
    midv = jnp.where(lane < live_mid, rbuf[0:1], -1)
    lowv = jnp.where(lane < live_low, rbuf[1:2], -1)
    eye = lax.broadcasted_iota(I32, (RK, S), 0) + tile * RK == lax.broadcasted_iota(I32, (RK, S), 1)

    def mid_onehot(b):
        pos = lax.broadcasted_iota(I32, (WIN, BLK), 0) + b * BLK
        qoh[b] = (pos == midv[:, b * BLK : (b + 1) * BLK]).astype(F32).astype(BF)

    def low_start(p):
        return p * PL // 128 * 128

    def low_onehot(p):
        pos = lax.broadcasted_iota(I32, (WIN, PL), 0) + low_start(p)
        roh[p] = (pos == lowv[:, p * PL : (p + 1) * PL]).astype(F32).astype(BF)

    def rows_without_transfer():
        u[BOT : BOT + RB, S:] = (lax.broadcasted_iota(I32, (RB, M), 0) + tile * RB == midv).astype(F32).astype(BF)
        dhi, dlo = split(dbuf[...])
        u[DI : DI + RK, :S] = dhi
        u[ID : ID + RK, :S] = eye.astype(F32).astype(BF)
        u[DIL : DIL + RK, :S] = dlo
        for r0, n in ((DI, 2 * RK), (BOTL, RB + RK)):
            u[r0 : r0 + n, S:] = jnp.zeros((n, M), BF)

    def choose(ys):
        for dx in range(NX):
            pm = jnp.broadcast_to(pmbuf[lax.rem(x + dx, NX)][0:1], (CB, RB))
            got = jnp.where(
                pm < 2,
                jnp.where(pm == 0, ygath[ys, 0], ygath[ys, 1]),
                jnp.where(pm == 2, ygath[ys, 2], ygath[ys, 3]),
            )
            if dx == 0:
                covsel[x * NY + ys] = got
            else:
                stage[dx - 1, ys] = got
                send(stage.at[dx - 1, ys], covsel.at[x * NY + ys], x_send, x_recv, (leaf_at(dx, 0), tile))

    def pass_on(a, s):
        for t in (zt(-s), zt(s)):
            send(whole[a].at[t], whole[a].at[t], c_send, c_recv.at[a, s], (leaf, sibling))

    def parent_columns():
        wait(covsel.at[pl.ds(0, (NX - 1) * NY)], x_recv)
        for m in range(F // 128):
            hi, lo = split(covsel[2 * m : 2 * m + 2].reshape(128, RB).T)
            csrc[:RB, m * 128 : (m + 1) * 128] = hi
            csrc[RB:, m * 128 : (m + 1) * 128] = lo
        for b in range(NB):
            got = dot(csrc[:, b * BLK : b * BLK + WIN], qoh[b]).astype(BF)
            u[TOP : TOP + RB, S + b * BLK : S + (b + 1) * BLK] = got[:RB]
            u[TOPL : TOPL + RB, S + b * BLK : S + (b + 1) * BLK] = got[RB:]

    def pick(p):
        v[p] = dot(u[:, low_start(p) : low_start(p) + WIN], roh[p]).astype(BF)

    def chip_rows(a, s):
        return (z,) if s == 0 else (lax.rem(z + s, NZ),) if s == 4 else (lax.rem(z + NZ - s, NZ), lax.rem(z + s, NZ))

    def come_from_sibling(a, s):
        wait(whole[a].at[pl.ds(0, 2 if 0 < s < 4 else 1)], c_recv.at[a, s])

    def mid_halves(s):
        come_from_sibling(0, s)
        for p in chip_rows(0, s):
            hi, lo = split(xm[pl.ds(p * NC, NC)].reshape(PL, S))
            fhi[pl.ds(p * PL, PL)] = hi
            flo[pl.ds(p * PL, PL)] = lo

    def low_terms(s):
        come_from_sibling(1, s)
        for p in chip_rows(1, s):
            hi, lo = split(xl[pl.ds(p * NC, NC)].reshape(PL, S))
            left = v[p]
            first, second = dot(left, hi), dot(left[:TOPL], lo)
            yhi[...] = first if s == 0 else yhi[...] + first
            ylo[...] = second if s == 0 else ylo[...] + second

    def cross_rows():
        both = dot(u[: 2 * RB, S:], fhi[...]) + dot(u[: 2 * RB, S:], flo[...])
        cross = both[:RB] + dot(u[TOPL : TOPL + RB, S:], fhi[...])
        mine = both[RB:]
        part = jnp.sum(cross * mine, axis=0, keepdims=True) + jnp.sum(jnp.where(eye, dbuf[...], 0.0), axis=0, keepdims=True)
        for k in range(4):
            fin[tile, k : k + 1] = part[:, k * 128 : (k + 1) * 128]
        for r0, rl, val in ((TOP, TOPL, cross), (BOT, BOTL, mine)):
            hi, lo = split(-val)
            u[r0 : r0 + RB, :S] = hi
            u[rl : rl + RB, :S] = lo

    rows_without_transfer()
    wait(pmbuf.at[pl.ds(0, 3)], p_recv)
    choose(y)

    todo = [[] for _ in range(NPIECE)]

    def at(k, f, *args):
        todo[k].append((f, args))

    for b in range(NB):
        at(b // 3, mid_onehot, b)
    for p in range(NZ):
        at(2 + p // 4, low_onehot, p)
    at(4, mid_halves, 0)
    at(5, mid_halves, 1)
    at(7, mid_halves, 2)
    at(7, parent_columns)
    for p in range(3, NZ):
        at(8, pick, p)
    at(9, mid_halves, 3)
    at(10, mid_halves, 4)
    at(10, cross_rows)
    for p in range(3):
        at(11, pick, p)
    at(11, low_terms, 0)
    at(12, low_terms, 1)
    at(12, low_terms, 2)
    at(13, low_terms, 3)
    at(13, low_terms, 4)

    ny = 7
    jy = 0
    for k in range(NPIECE):
        while jy < ny and jy <= k:
            for d in (0, 1):
                y_come(d, jy)
                if jy + 2 < ny:
                    y_go(d, jy + 2)
            s, p = divmod(jy, 2)
            if s < 3 and p == 1:
                choose(lax.rem(y + NY - 1 - s, NY))
                choose(lax.rem(y + s + 1, NY))
            elif jy == ny - 1:
                choose(lax.rem(y + NY // 2, NY))
            jy += 1
        a, s = UP[k][:2]
        for d in (0, 1):
            z_come(d, k)
            for q in due[d].get(k, ()):
                z_go(d, q)
            if s == 3:
                half = whole[a].at[zt(4), pl.ds((UP, DOWN)[d][k][2], RF // 2)]
                send(half, half, c_send, c_recv.at[a, 4], (leaf, sibling))
        if s < 3 and UP[k + 1][:2] != (a, s):
            pass_on(a, s + 1)
        for f, args in todo[k]:
            f(*args)

    def rows(r0, rl, n):
        return yhi[r0 : r0 + n] + yhi[rl : rl + n] + ylo[r0 : r0 + n]

    part = jnp.sum(rows(TOP, TOPL, RB) * rows(BOT, BOTL, RB), axis=0, keepdims=True)
    part += jnp.sum(rows(DI, DIL, RK) * (yhi[ID : ID + RK] + ylo[ID : ID + RK]), axis=0, keepdims=True)
    for k in range(4):
        fin[tile, k + 4 : k + 5] = part[:, k * 128 : (k + 1) * 128]

    for d in sorted(range(1, NT), key=lambda d: -min(d, NT - d)):
        send(fin.at[tile], fin.at[tile], f_send, f_recv, (leaf, lax.rem(tile + d, NT)))
    wait(fin.at[pl.ds(0, NT - 1)], f_recv)
    total = jnp.sum(fin[...], axis=0)
    per = 128 // RK
    row = lax.broadcasted_iota(I32, (8, 128), 0)
    turn = lax.rem(128 - lax.rem(tile, per) * RK, 128)
    for o, base, add in ((0, 0, None), (1, 4, lbuf)):
        line = jnp.sum(jnp.where(row == base + tile // per, total, 0.0), axis=0, keepdims=True)
        line = pltpu.roll(jnp.broadcast_to(line, (8, 128)), turn, 1)[0:1, :RK]
        out[o : o + 1] = line if add is None else line + add[...]

    wait(fin.at[pl.ds(0, NT - 1)], f_send)
    wait(pmbuf.at[pl.ds(0, 3)], p_send)
    wait(ygath.at[pl.ds(0, NY - 1)], y_send)
    wait(stage, x_send)
    for w in whole:
        wait(w.at[pl.ds(0, NZ - 1)], z_send)
        wait(w.at[pl.ds(0, NZ)], c_send)


def body(parent_cov, parent_map, front_rows, rows_mid, rows_low, factor_mid, dinv_mid, factor_low, diag_low):
    vm, hb = (pl.BlockSpec(memory_space=s) for s in (pltpu.VMEM, pl.ANY))
    dma = pltpu.SemaphoreType.DMA
    out = pl.pallas_call(
        kernel,
        out_shape=jax.ShapeDtypeStruct((2, RK), F32),
        in_specs=[hb] * 9,
        out_specs=vm,
        scratch_shapes=[
            pltpu.VMEM((NY, NP, CB, RB), F32),
            pltpu.VMEM((NX - 1, NY, CB, RB), F32),
            pltpu.VMEM((NL, CB, RB), F32),
            pltpu.VMEM((NX, 8, 128), I32),
            pltpu.VMEM((NT, RF, S), F32),
            pltpu.VMEM((NT, RF, S), F32),
            pltpu.VMEM((2, M), I32),
            pltpu.VMEM((RK, S), F32),
            pltpu.VMEM((1, RK), F32),
            pltpu.VMEM((NB, WIN, BLK), BF),
            pltpu.VMEM((NZ, WIN, PL), BF),
            pltpu.VMEM((2 * RB, F), BF),
            pltpu.VMEM((ROWS, F), BF),
            pltpu.VMEM((NZ, ROWS, PL), BF),
            pltpu.VMEM((M, S), BF),
            pltpu.VMEM((M, S), BF),
            pltpu.VMEM((ROWS, S), F32),
            pltpu.VMEM((TOPL, S), F32),
            pltpu.VMEM((NT, 8, 128), F32),
            pltpu.SMEM((1,), I32),
            pltpu.SMEM((1, 2), I32),
            dma, dma((2, 14)), dma, dma, dma, dma, dma, dma((2, NPIECE)), dma, dma((2, 5)), dma, dma, dma((9,)),
        ],
        compiler_params=pltpu.CompilerParams(
            collective_id=0, has_side_effects=True, vmem_limit_bytes=60 * 1024 * 1024
        ),
        cost_estimate=pl.CostEstimate(flops=5 * 10**9, bytes_accessed=10**6, transcendentals=0),
    )(
        parent_map, front_rows, jnp.swapaxes(parent_cov, 1, 2), rows_mid, rows_low,
        factor_mid[0], dinv_mid[0], factor_low[0], diag_low,
    )
    return out[0:1], out[1:2]


def solution(mesh):
    return jax.shard_map(
        body,
        mesh=mesh,
        in_specs=(
            P(None, "tile", "leaf"),
            P("leaf"),
            P("leaf", None),
            P("leaf", None),
            P("leaf", None),
            P("leaf", "tile", None),
            P("leaf", "tile", None),
            P("leaf", "tile", None),
            P("leaf", "tile"),
        ),
        out_specs=(P("leaf", "tile"), P("leaf", "tile")),
        check_vma=False,
    )
```

```python
import jax
import jax.numpy as jnp
from jax import lax
from jax.experimental import pallas as pl
from jax.experimental.pallas import tpu as pltpu
from jax.sharding import PartitionSpec as P

NX, NY, NZ, NC = 4, 8, 8, 2
NT, NL = NZ * NC, NX * NY
NP, S, M, F = 4, 512, 1536, 2048
RB = F // NT
RF = M // NT
RK = S // NT
CB = F // NL
PL = NC * RF
WIN, BLK = 768, 256
NB = M // BLK
BF, F32, I32 = jnp.bfloat16, jnp.float32, jnp.int32
MESH = pl.DeviceIdType.MESH
AHEAD, LAG = 4, 1

TOP, BOT, DI, ID, TOPL, BOTL, DIL, ROWS = 0, RB, 2 * RB, 2 * RB + RK, 2 * RB + 2 * RK, 3 * RB + 2 * RK, 4 * RB + 2 * RK, 4 * RB + 3 * RK


def ring_order():
    def pieces(a, s):
        if s < 3:
            return [(a, s, 0, 48), (a, s, 48, 48)]
        return [(a, s, 0, 48)]

    up = []
    for s in range(4 + LAG):
        up += (pieces(0, s) if s < 4 else []) + (pieces(1, s - LAG) if s >= LAG else [])
    down = [(a, s, RF - r - n, n) for a, s, r, n in up]
    return up, down


UP, DOWN = ring_order()
NPIECE = len(UP)


def source_of(seq, k):
    a, s, r, n = seq[k]
    return next(i for i, (b, q, r0, m) in enumerate(seq) if b == a and q == s - 1 and r0 <= r and r + n <= r0 + m)


def split(v):
    hi = v.astype(BF)
    return hi, (v - hi.astype(F32)).astype(BF)


def dot(a, b):
    return jnp.dot(a, b, preferred_element_type=F32)


def kernel(
    pmap_hbm, counts_hbm, cov, rows_mid, rows_low, fm, dinv, fl, dlow,
    out,
    ygath, stage, covsel, pmbuf, xm, xl, rbuf, dbuf, lbuf, qoh, roh, csrc, u, v, fhi, flo, yhi, fin, pmap, counts,
    y_send, y_recv, x_send, x_recv, p_send, p_recv, z_send, z_recv, c_send, c_recv, f_send, f_recv, l_sem,
):
    leaf, tile = lax.axis_index("leaf"), lax.axis_index("tile")
    x, y = leaf // NY, leaf % NY
    z, c = tile // NC, tile % NC

    def leaf_at(dx, dy):
        return lax.rem(x + dx + NX, NX) * NY + lax.rem(y + dy + NY, NY)

    def zt(dz):
        return lax.rem(z + dz + NZ, NZ) * NC + c

    sibling = z * NC + (1 - c)
    up, down = zt(1), zt(-1)
    ynext, yprev = leaf_at(0, 1), leaf_at(0, -1)
    own, whole = (fm, fl), (xm, xl)

    barrier = pltpu.get_barrier_semaphore()
    near = [(leaf, up), (leaf, down), (leaf, sibling), (ynext, tile), (yprev, tile)]
    near += [(leaf_at(dx, 0), tile) for dx in (1, 2, 3)]
    for other in near:
        pl.semaphore_signal(barrier, inc=1, device_id=other, device_id_type=MESH)

    parent = pltpu.make_async_copy(pmap_hbm, pmap, l_sem.at[8])
    parent.start()
    local = [
        (cov, ygath.at[y]), (rows_mid, rbuf.at[0:1]), (rows_low, rbuf.at[1:2]), (dinv, dbuf), (dlow, lbuf),
        (counts_hbm, counts), (fm, xm.at[tile]), (fl, xl.at[tile]),
    ]
    local = [pltpu.make_async_copy(src, dst, l_sem.at[i]) for i, (src, dst) in enumerate(local)]
    pl.semaphore_wait(barrier, len(near))

    def send(src, dst, ssem, rsem, where):
        pltpu.make_async_remote_copy(
            src_ref=src, dst_ref=dst, send_sem=ssem, recv_sem=rsem, device_id=where, device_id_type=MESH
        ).start()

    def wait(ref, sem):
        pltpu.make_async_copy(ref, ref, sem).wait()

    def y_piece(d, j):
        s, p = divmod(j, 2)
        return s, pl.ds(2 * (p if d == 0 else 1 - p), 2)

    def y_go(d, j):
        s, p = y_piece(d, j)
        src_y = lax.rem(y + (NY - s if d == 0 else s), NY)
        dst = ygath.at[src_y, p]
        send(cov.at[p] if s == 0 else dst, dst, y_send, y_recv.at[d, j], (ynext if d == 0 else yprev, tile))

    def y_come(d, j):
        s, p = y_piece(d, j)
        wait(ygath.at[lax.rem(y + (NY - 1 - s if d == 0 else s + 1), NY), p], y_recv.at[d, j])

    def z_go(d, k):
        a, s, r, n = (UP, DOWN)[d][k]
        dst = whole[a].at[zt(-s if d == 0 else s), pl.ds(r, n)]
        send(own[a].at[pl.ds(r, n)] if s == 0 else dst, dst, z_send, z_recv.at[d, k], (leaf, up if d == 0 else down))

    def z_come(d, k):
        a, s, r, n = (UP, DOWN)[d][k]
        wait(whole[a].at[zt(-s - 1 if d == 0 else s + 1), pl.ds(r, n)], z_recv.at[d, k])

    due = ({}, {})
    for k in range(NPIECE):
        for d, seq in ((0, UP), (1, DOWN)):
            after = k - AHEAD if seq[k][1] == 0 else max(k - AHEAD, source_of(seq, k))
            if after < 0:
                z_go(d, k)
            else:
                due[d].setdefault(after, []).append(k)
    for j in range(2):
        y_go(0, j)
        y_go(1, j)
    parent.wait()
    pmbuf[x] = jnp.full((8, 128), pmap[0], I32)
    for dx in (1, 2, 3):
        send(pmbuf.at[x], pmbuf.at[x], p_send, p_recv, (leaf_at(dx, 0), tile))
    for copy in local:
        copy.start()
    for a in range(2):
        send(own[a], whole[a].at[tile], c_send, c_recv.at[a, 0], (leaf, sibling))

    for copy in local:
        copy.wait()
    live_mid, live_low = counts[0, 0], counts[0, 1]
    lane = lax.broadcasted_iota(I32, (1, M), 1)
    midv = jnp.where(lane < live_mid, rbuf[0:1], -1)
    lowv = jnp.where(lane < live_low, rbuf[1:2], -1)
    eye = lax.broadcasted_iota(I32, (RK, S), 0) + tile * RK == lax.broadcasted_iota(I32, (RK, S), 1)

    def mid_onehot(b):
        pos = lax.broadcasted_iota(I32, (WIN, BLK), 0) + b * BLK
        qoh[b] = (pos == midv[:, b * BLK : (b + 1) * BLK]).astype(F32).astype(BF)

    def low_start(p):
        return p * PL // 128 * 128

    def low_onehot(p):
        pos = lax.broadcasted_iota(I32, (WIN, PL), 0) + low_start(p)
        roh[p] = (pos == lowv[:, p * PL : (p + 1) * PL]).astype(F32).astype(BF)

    def rows_without_transfer():
        u[BOT : BOT + RB, S:] = (lax.broadcasted_iota(I32, (RB, M), 0) + tile * RB == midv).astype(F32).astype(BF)
        dhi, dlo = split(dbuf[...])
        u[DI : DI + RK, :S] = dhi
        u[ID : ID + RK, :S] = eye.astype(F32).astype(BF)
        u[DIL : DIL + RK, :S] = dlo
        for r0, n in ((DI, 2 * RK), (BOTL, RB + RK)):
            u[r0 : r0 + n, S:] = jnp.zeros((n, M), BF)

    def choose(ys):
        for dx in range(NX):
            pm = jnp.broadcast_to(pmbuf[lax.rem(x + dx, NX)][0:1], (CB, RB))
            got = jnp.where(
                pm < 2,
                jnp.where(pm == 0, ygath[ys, 0], ygath[ys, 1]),
                jnp.where(pm == 2, ygath[ys, 2], ygath[ys, 3]),
            )
            if dx == 0:
                covsel[x * NY + ys] = got
            else:
                stage[dx - 1, ys] = got
                send(stage.at[dx - 1, ys], covsel.at[x * NY + ys], x_send, x_recv, (leaf_at(dx, 0), tile))

    def pass_on(a, s):
        for t in (zt(-s), zt(s)):
            send(whole[a].at[t], whole[a].at[t], c_send, c_recv.at[a, s], (leaf, sibling))

    def parent_columns():
        wait(covsel.at[pl.ds(0, (NX - 1) * NY)], x_recv)
        for m in range(F // 128):
            hi, lo = split(covsel[2 * m : 2 * m + 2].reshape(128, RB).T)
            csrc[:RB, m * 128 : (m + 1) * 128] = hi
            csrc[RB:, m * 128 : (m + 1) * 128] = lo
        for b in range(NB):
            got = dot(csrc[:, b * BLK : b * BLK + WIN], qoh[b]).astype(BF)
            u[TOP : TOP + RB, S + b * BLK : S + (b + 1) * BLK] = got[:RB]
            u[TOPL : TOPL + RB, S + b * BLK : S + (b + 1) * BLK] = got[RB:]

    def pick(p):
        v[p] = dot(u[:, low_start(p) : low_start(p) + WIN], roh[p]).astype(BF)

    def chip_rows(a, s):
        return (z,) if s == 0 else (lax.rem(z + s, NZ),) if s == 4 else (lax.rem(z + NZ - s, NZ), lax.rem(z + s, NZ))

    def come_from_sibling(a, s):
        wait(whole[a].at[pl.ds(0, 2 if 0 < s < 4 else 1)], c_recv.at[a, s])

    def mid_halves(s):
        come_from_sibling(0, s)
        for p in chip_rows(0, s):
            hi, lo = split(xm[pl.ds(p * NC, NC)].reshape(PL, S))
            fhi[pl.ds(p * PL, PL)] = hi
            flo[pl.ds(p * PL, PL)] = lo

    def low_terms(s):
        come_from_sibling(1, s)
        for p in chip_rows(1, s):
            hi, lo = split(xl[pl.ds(p * NC, NC)].reshape(PL, S))
            left = v[p]
            first, second = dot(left, hi), dot(left[:TOPL], lo)
            for r0, add in ((0, first[:TOPL] + second), (TOPL, first[TOPL:])):
                part = slice(r0, r0 + add.shape[0])
                yhi[part] = add if s == 0 else yhi[part] + add

    def cross_rows():
        both = dot(u[: 2 * RB, S:], fhi[...]) + dot(u[: 2 * RB, S:], flo[...])
        cross = both[:RB] + dot(u[TOPL : TOPL + RB, S:], fhi[...])
        mine = both[RB:]
        part = jnp.sum(cross * mine, axis=0, keepdims=True) + jnp.sum(jnp.where(eye, dbuf[...], 0.0), axis=0, keepdims=True)
        for k in range(4):
            fin[tile, k : k + 1] = part[:, k * 128 : (k + 1) * 128]
        for r0, rl, val in ((TOP, TOPL, cross), (BOT, BOTL, mine)):
            hi, lo = split(-val)
            u[r0 : r0 + RB, :S] = hi
            u[rl : rl + RB, :S] = lo

    rows_without_transfer()
    wait(pmbuf.at[pl.ds(0, 3)], p_recv)
    choose(y)

    todo = [[] for _ in range(NPIECE)]

    def at(k, f, *args):
        todo[k].append((f, args))

    for b in range(NB):
        at(b // 2, mid_onehot, b)
    for p in range(NZ):
        at(2 + p // 2, low_onehot, p)
    at(4, mid_halves, 0)
    at(5, mid_halves, 1)
    at(7, mid_halves, 2)
    at(7, parent_columns)
    for p in range(3, NZ):
        at(8, pick, p)
    at(9, mid_halves, 3)
    at(10, mid_halves, 4)
    at(10, cross_rows)
    for p in range(3):
        at(11, pick, p)
    at(11, low_terms, 0)
    at(12, low_terms, 1)
    at(12, low_terms, 2)
    at(13, low_terms, 3)
    at(13, low_terms, 4)

    ny = 7
    jy = 0
    for k in range(NPIECE):
        while jy < ny and jy <= k:
            for d in (0, 1):
                y_come(d, jy)
                if jy + 2 < ny:
                    y_go(d, jy + 2)
            s, p = divmod(jy, 2)
            if s < 3 and p == 1:
                choose(lax.rem(y + NY - 1 - s, NY))
                choose(lax.rem(y + s + 1, NY))
            elif jy == ny - 1:
                choose(lax.rem(y + NY // 2, NY))
            jy += 1
        a, s = UP[k][:2]
        for d in (0, 1):
            z_come(d, k)
            for q in due[d].get(k, ()):
                z_go(d, q)
            if s == 3:
                half = whole[a].at[zt(4), pl.ds((UP, DOWN)[d][k][2], RF // 2)]
                send(half, half, c_send, c_recv.at[a, 4], (leaf, sibling))
        if s < 3 and UP[k + 1][:2] != (a, s):
            pass_on(a, s + 1)
        for f, args in todo[k]:
            f(*args)

    def rows(r0, rl, n):
        return yhi[r0 : r0 + n] + yhi[rl : rl + n]

    part = jnp.sum(rows(TOP, TOPL, RB) * rows(BOT, BOTL, RB), axis=0, keepdims=True)
    part += jnp.sum(rows(DI, DIL, RK) * yhi[ID : ID + RK], axis=0, keepdims=True)
    for k in range(4):
        fin[tile, k + 4 : k + 5] = part[:, k * 128 : (k + 1) * 128]

    for d in sorted(range(1, NT), key=lambda d: -min(d, NT - d)):
        send(fin.at[tile], fin.at[tile], f_send, f_recv, (leaf, lax.rem(tile + d, NT)))
    wait(fin.at[pl.ds(0, NT - 1)], f_recv)
    total = jnp.sum(fin[...], axis=0)
    per = 128 // RK
    row = lax.broadcasted_iota(I32, (8, 128), 0)
    turn = lax.rem(128 - lax.rem(tile, per) * RK, 128)
    for o, base, add in ((0, 0, None), (1, 4, lbuf)):
        line = jnp.sum(jnp.where(row == base + tile // per, total, 0.0), axis=0, keepdims=True)
        line = pltpu.roll(jnp.broadcast_to(line, (8, 128)), turn, 1)[0:1, :RK]
        out[o : o + 1] = line if add is None else line + add[...]

    wait(fin.at[pl.ds(0, NT - 1)], f_send)
    wait(pmbuf.at[pl.ds(0, 3)], p_send)
    wait(ygath.at[pl.ds(0, NY - 1)], y_send)
    wait(stage, x_send)
    for w in whole:
        wait(w.at[pl.ds(0, NZ - 1)], z_send)
        wait(w.at[pl.ds(0, NZ)], c_send)


def body(parent_cov, parent_map, front_rows, rows_mid, rows_low, factor_mid, dinv_mid, factor_low, diag_low):
    vm, hb = (pl.BlockSpec(memory_space=s) for s in (pltpu.VMEM, pl.ANY))
    dma = pltpu.SemaphoreType.DMA
    out = pl.pallas_call(
        kernel,
        out_shape=jax.ShapeDtypeStruct((2, RK), F32),
        in_specs=[hb] * 9,
        out_specs=vm,
        scratch_shapes=[
            pltpu.VMEM((NY, NP, CB, RB), F32),
            pltpu.VMEM((NX - 1, NY, CB, RB), F32),
            pltpu.VMEM((NL, CB, RB), F32),
            pltpu.VMEM((NX, 8, 128), I32),
            pltpu.VMEM((NT, RF, S), F32),
            pltpu.VMEM((NT, RF, S), F32),
            pltpu.VMEM((2, M), I32),
            pltpu.VMEM((RK, S), F32),
            pltpu.VMEM((1, RK), F32),
            pltpu.VMEM((NB, WIN, BLK), BF),
            pltpu.VMEM((NZ, WIN, PL), BF),
            pltpu.VMEM((2 * RB, F), BF),
            pltpu.VMEM((ROWS, F), BF),
            pltpu.VMEM((NZ, ROWS, PL), BF),
            pltpu.VMEM((M, S), BF),
            pltpu.VMEM((M, S), BF),
            pltpu.VMEM((ROWS, S), F32),
            pltpu.VMEM((NT, 8, 128), F32),
            pltpu.SMEM((1,), I32),
            pltpu.SMEM((1, 2), I32),
            dma, dma((2, 14)), dma, dma, dma, dma, dma, dma((2, NPIECE)), dma, dma((2, 5)), dma, dma, dma((9,)),
        ],
        compiler_params=pltpu.CompilerParams(
            collective_id=0, has_side_effects=True, vmem_limit_bytes=60 * 1024 * 1024
        ),
        cost_estimate=pl.CostEstimate(flops=5 * 10**9, bytes_accessed=10**6, transcendentals=0),
    )(
        parent_map, front_rows, jnp.swapaxes(parent_cov, 1, 2), rows_mid, rows_low,
        factor_mid[0], dinv_mid[0], factor_low[0], diag_low,
    )
    return out[0:1], out[1:2]


def solution(mesh):
    return jax.shard_map(
        body,
        mesh=mesh,
        in_specs=(
            P(None, "tile", "leaf"),
            P("leaf"),
            P("leaf", None),
            P("leaf", None),
            P("leaf", None),
            P("leaf", "tile", None),
            P("leaf", "tile", None),
            P("leaf", "tile", None),
            P("leaf", "tile"),
        ),
        out_specs=(P("leaf", "tile"), P("leaf", "tile")),
        check_vma=False,
    )
```
